32 devices in a mesh: samples: 8 (over z, y), vblocks: 4 (over x, core).
Axes of the slice: x: 2, y: 2, z: 4, core: 2. Of those that a mesh axis runs over, the one named last changes fastest.
Arguments:
- genotypes: int32 [8192, 4096], P('samples', 'vblocks'), may hold values from 0 to 2
- typed_mask: int32 [4096], P('vblocks'), may hold values 0 or 1
- z_scores: float32 [128, 4096], P('samples', 'vblocks'), may hold values from -60 to 60
Outputs:
- solution: float32 [128, 4096], P('samples', 'vblocks')
- imputed: float32 [128, 4096], P('samples', 'vblocks')
The draws below stay inside these ranges and needn't reach their ends.
All inputs are finite; a program needn't handle non-finite values. No bound on the sum of `typed_mask` on one device may be relied on, other than what follows from the above.
Results may differ from the reference program's by a relative error of at most 0.0068.
Values may be sent and summed in bfloat16 or wider, within the bound.
A program may use at most 64 MiB of HBM per device.

```python
import math
import jax
import jax.numpy as jnp
from jax import lax

BAND = 1024
ITERS = 3
S = 8192
V = 4096
K = 128
N_VBLOCKS = 4


def haplotype(key_hap, thresholds):
    key_draw, key_copy = jax.random.split(key_hap)
    uniform_draw = jax.random.randint(key_draw, (S, V), 0, 100)
    copied = jax.random.randint(key_copy, (S, V), 0, 10) < 9
    position = lax.broadcasted_iota(jnp.int32, (S, V), 1)
    fresh_start = jnp.logical_or(jnp.logical_not(copied), position == 0)
    source = lax.cummax(jnp.where(fresh_start, position, 0), axis=1)
    carried = jnp.take_along_axis(uniform_draw, source, axis=1)
    return (carried < thresholds).astype(jnp.int32)


def draw_genotypes(key, part):
    key_freq, key_first, key_second = jax.random.split(key, 3)
    percent = jax.random.randint(key_freq, (V,), 1, 34)
    sample_index = lax.broadcasted_iota(jnp.int32, (S, V), 0)
    thresholds = percent[None, :] * (S + 2 * sample_index) // S
    return haplotype(key_first, thresholds) + haplotype(key_second, thresholds)


def draw_z_scores(key, part):
    key_base, key_rows, key_cols = jax.random.split(key, 3)
    spread = math.log(10.0) / 2.0
    row_scale = jnp.exp(jax.random.uniform(key_rows, (1, V), jnp.float32, -spread, spread))
    col_scale = jnp.exp(jax.random.uniform(key_cols, (K, 1), jnp.float32, -spread, spread))
    base_draw = jax.random.truncated_normal(key_base, -6.0, 6.0, (K, V), jnp.float32)
    return (base_draw * row_scale * col_scale).astype(jnp.float32)


def touch_ends(array, rng, smallest, largest):
    index_at = [jax.random.randint(jax.random.fold_in(rng, axis), (), 0, length) for axis, length in enumerate(array.shape)]
    main_axis = array.shape.index(max(array.shape))
    neighbour = index_at[:main_axis] + [(index_at[main_axis] + 1) % array.shape[main_axis]] + index_at[main_axis + 1:]
    return array.at[tuple(index_at)].set(smallest).at[tuple(neighbour)].set(largest)


def setup_inputs(seed: int = 0) -> dict:
    keys = jax.random.split(jax.random.key(seed), 4)
    genotypes = draw_genotypes(jax.random.fold_in(keys[3], 71), 0)
    typed_mask = touch_ends((jax.random.randint(keys[1], (V,), 0, 4) < 3).astype(jnp.int32), jax.random.fold_in(keys[1], 1), 0, 1)
    z_scores = draw_z_scores(jax.random.fold_in(keys[3], 71), 0)
    return dict(genotypes=genotypes, typed_mask=typed_mask, z_scores=z_scores)


RIDGE = 0.1
EPSILON = 1e-05
HIGHEST = lax.Precision.HIGHEST

def contract_rows(first_mat, second_mat):
    return lax.dot_general(first_mat, second_mat, (((0,), (0,)), ((), ())), preferred_element_type=jnp.float32)

def times_transpose(vector, matrix):
    return lax.dot_general(vector, matrix, (((1,), (1,)), ((), ())), precision=HIGHEST, preferred_element_type=jnp.float32)

def apply_link(vector, own_blocks, edge_blocks):
    pieces = [vector[:, block_index * BAND:(block_index + 1) * BAND] for block_index in range(N_VBLOCKS)]
    outputs = []
    for block_index in range(N_VBLOCKS):
        result = times_transpose(pieces[block_index], own_blocks[block_index])
        if block_index + 1 < N_VBLOCKS:
            result = result + 0.5 * times_transpose(pieces[block_index + 1], edge_blocks[block_index])
        if block_index > 0:
            result = result + 0.5 * jnp.dot(pieces[block_index - 1], edge_blocks[block_index - 1], precision=HIGHEST, preferred_element_type=jnp.float32)
        outputs.append(result)
    return jnp.concatenate(outputs, axis=1)

def rounded_link(first_mat, second_mat, samples):
    summed = (contract_rows(first_mat, second_mat) / samples).astype(jnp.bfloat16)
    return lax.optimization_barrier(summed).astype(jnp.float32)

def reference(genotypes, typed_mask, z_scores):
    samples = genotypes.shape[0]
    standard_blocks = []
    for block_index in range(N_VBLOCKS):
        dosage = genotypes[:, block_index * BAND:(block_index + 1) * BAND].astype(jnp.float32)
        totals = lax.optimization_barrier(jnp.sum(dosage, axis=0))
        squares = lax.optimization_barrier(jnp.sum(dosage * dosage, axis=0))
        mean_dosage = totals / samples
        variance = squares / samples - mean_dosage * mean_dosage
        standard_blocks.append(((dosage - mean_dosage) * lax.rsqrt(variance + EPSILON)).astype(jnp.bfloat16))
    own_blocks = []
    edge_blocks = []
    for block_index in range(N_VBLOCKS):
        own_blocks.append(rounded_link(standard_blocks[block_index], standard_blocks[block_index], samples))
        if block_index + 1 < N_VBLOCKS:
            edge_blocks.append(rounded_link(standard_blocks[block_index], standard_blocks[block_index + 1], samples))
        else:
            edge_blocks.append(jnp.zeros((BAND, BAND), jnp.float32))
    mask_row = typed_mask.astype(jnp.float32)[None, :]

    def operator(vector):
        return mask_row * apply_link(mask_row * vector, own_blocks, edge_blocks) + RIDGE * vector
    right_side = mask_row * z_scores
    solution = jnp.zeros_like(right_side)
    residual = right_side
    direction = right_side
    norm_now = lax.optimization_barrier(jnp.sum(residual * residual, axis=1))
    for iteration in range(ITERS):
        image = operator(direction)
        step_size = norm_now / lax.optimization_barrier(jnp.sum(direction * image, axis=1))
        solution = solution + step_size[:, None] * direction
        residual = residual - step_size[:, None] * image
        if iteration + 1 < ITERS:
            norm_next = lax.optimization_barrier(jnp.sum(residual * residual, axis=1))
            direction = residual + (norm_next / norm_now)[:, None] * direction
            norm_now = norm_next
    projected = apply_link(mask_row * solution, own_blocks, edge_blocks)
    imputed = jnp.where(typed_mask[None, :] == 1, z_scores, projected)
    return (solution, imputed)
```

```python
import functools

import jax
import jax.numpy as jnp
from jax import lax
from jax.experimental import pallas as pl
from jax.experimental.pallas import tpu as pltpu
from jax.sharding import PartitionSpec as P

ITERS = 3
RIDGE = 0.1
EPSILON = 1e-05
MESH = pl.DeviceIdType.MESH
ROWS = 256
TRAITS = 128
LANES = 128


def loop(count, body):
    if count <= 4:
        for index in range(count):
            body(index)
    else:
        lax.fori_loop(0, count, lambda index, carry: (body(index), carry)[1], 0)


def split_high_low(value):
    high = value.astype(jnp.bfloat16)
    low = (value - high.astype(jnp.float32)).astype(jnp.bfloat16)
    return jnp.concatenate([high, low], axis=0)


def kernel(
    n,
    nv,
    g_hbm,
    mask_ref,
    z_ref,
    sol_ref,
    imp_ref,
    g_buf,
    x_ref,
    stat,
    u_all,
    t_own,
    t_side,
    p_acc,
    p_send,
    p_recv,
    dots,
    g_sem,
    stat_ss,
    stat_rs,
    u_ss,
    u_rs,
    t_ss,
    t_rs,
    p_ss,
    p_rs,
    dot_ss,
    dot_rs,
):
    me = lax.axis_index("samples")
    mv = lax.axis_index("vblocks")
    tiles, _, width = g_buf.shape
    kd = z_ref.shape[0]
    chunks = (n * kd) // TRAITS
    per_chunk = TRAITS // kd
    packs = width // LANES
    total_samples = float(n * tiles * ROWS)

    for c in range(tiles):
        pltpu.make_async_copy(
            g_hbm.at[pl.ds(c * ROWS, ROWS)], g_buf.at[c], g_sem.at[c]
        ).start()

    barrier = pltpu.get_barrier_semaphore()

    def greet_samples(i):
        peer = lax.rem(me + i + 1, n)
        pl.semaphore_signal(barrier, inc=1, device_id=(peer, mv), device_id_type=MESH)

    def greet_blocks(i):
        peer = lax.rem(mv + i + 1, nv)
        pl.semaphore_signal(barrier, inc=1, device_id=(me, peer), device_id_type=MESH)

    loop(n - 1, greet_samples)
    loop(nv - 1, greet_blocks)

    def to_peer(buf, ss, rs, peer):
        return pltpu.make_async_remote_copy(
            src_ref=buf.at[me],
            dst_ref=buf.at[me],
            send_sem=ss.at[peer],
            recv_sem=rs.at[me],
            device_id=(peer, mv),
            device_id_type=MESH,
        )

    def from_peer(buf, ss, rs, peer):
        return pltpu.make_async_remote_copy(
            src_ref=buf.at[peer],
            dst_ref=buf.at[peer],
            send_sem=ss.at[peer],
            recv_sem=rs.at[peer],
            device_id=(peer, mv),
            device_id_type=MESH,
        )

    def each_peer(action):
        loop(n - 1, lambda i: action(lax.rem(me + i + 1, n)))

    totals = jnp.zeros((1, width), jnp.float32)
    squares = jnp.zeros((1, width), jnp.float32)
    for c in range(tiles):
        pltpu.make_async_copy(
            g_hbm.at[pl.ds(c * ROWS, ROWS)], g_buf.at[c], g_sem.at[c]
        ).wait()
        dosage = g_buf[c].astype(jnp.float32)
        totals = totals + jnp.sum(dosage, axis=0, keepdims=True)
        squares = squares + jnp.sum(dosage * dosage, axis=0, keepdims=True)
    for i in range(packs):
        stat[me, i : i + 1, :] = totals[:, i * LANES : (i + 1) * LANES]
        stat[me, packs + i : packs + i + 1, :] = squares[:, i * LANES : (i + 1) * LANES]
    mask_row = mask_ref[...].astype(jnp.float32)
    residual = mask_row * z_ref[...]
    u_all[me] = residual

    pl.semaphore_wait(barrier, n - 1 + nv - 1)
    each_peer(lambda q: to_peer(stat, stat_ss, stat_rs, q).start())
    each_peer(lambda q: to_peer(u_all, u_ss.at[0], u_rs.at[0], q).start())
    each_peer(lambda q: from_peer(stat, stat_ss, stat_rs, q).wait_recv())
    summed = jnp.sum(stat[...], axis=0)
    totals = jnp.concatenate([summed[i : i + 1] for i in range(packs)], axis=1)
    squares = jnp.concatenate([summed[packs + i : packs + i + 1] for i in range(packs)], axis=1)
    mean_dosage = totals / total_samples
    variance = squares / total_samples - mean_dosage * mean_dosage
    scale = lax.rsqrt(variance + EPSILON)
    for c in range(tiles):
        dosage = g_buf[c].astype(jnp.float32)
        x_ref[c] = ((dosage - mean_dosage) * scale).astype(jnp.bfloat16)
    each_peer(lambda q: to_peer(stat, stat_ss, stat_rs, q).wait_send())

    def t_copy(k, j, ahead):
        side = 0 if ahead else 1
        return pltpu.make_async_remote_copy(
            src_ref=t_own.at[j],
            dst_ref=t_side.at[side, j],
            send_sem=t_ss.at[k, side, j],
            recv_sem=t_rs.at[k, side, j],
            device_id=(me, mv + 1 if ahead else mv - 1),
            device_id_type=MESH,
        )

    @pl.when(mv == 0)
    def _():
        t_side[0] = jnp.zeros(t_side.shape[1:], t_side.dtype)

    @pl.when(mv == nv - 1)
    def _():
        t_side[1] = jnp.zeros(t_side.shape[1:], t_side.dtype)

    lane = lax.broadcasted_iota(jnp.int32, (kd, LANES), 1)

    def row_sums(first, second):
        return jnp.sum(first * second, axis=1, keepdims=True)

    direction = residual
    weights = jnp.zeros_like(residual)
    projected = jnp.zeros_like(residual)
    for k in range(ITERS):
        each_peer(lambda q: from_peer(u_all, u_ss.at[k], u_rs.at[k], q).wait_recv())

        def products(j):
            def one(c):
                u = u_all[pl.ds(c * per_chunk, per_chunk)].reshape(TRAITS, width)
                both = lax.dot_general(
                    split_high_low(u),
                    x_ref[j],
                    (((1,), (1,)), ((), ())),
                    preferred_element_type=jnp.float32,
                )
                t_own[j, pl.ds(pl.multiple_of(c * TRAITS, TRAITS), TRAITS)] = (
                    both[:TRAITS] + both[TRAITS:]
                ).astype(jnp.bfloat16)

            loop(chunks, one)

            @pl.when(mv < nv - 1)
            def _():
                t_copy(k, j, True).start()

            @pl.when(mv > 0)
            def _():
                t_copy(k, j, False).start()

        loop(tiles, products)

        def back(j):
            @pl.when(mv > 0)
            def _():
                t_copy(k, j, True).wait_recv()

            @pl.when(mv < nv - 1)
            def _():
                t_copy(k, j, False).wait_recv()

            def one(c):
                at = pl.ds(pl.multiple_of(c * TRAITS, TRAITS), TRAITS)
                mixed = t_own[j, at].astype(jnp.float32) + 0.5 * (
                    t_side[0, j, at].astype(jnp.float32) + t_side[1, j, at].astype(jnp.float32)
                )
                part = jnp.dot(
                    mixed.astype(jnp.bfloat16), x_ref[j], preferred_element_type=jnp.float32
                )
                if isinstance(j, int) and j == 0:
                    p_acc[at] = part
                else:
                    p_acc[at] = p_acc[at] + part

            loop(chunks, one)

        if tiles > 4:
            p_acc[...] = jnp.zeros_like(p_acc)
        loop(tiles, back)

        def to_send(c):
            at = pl.ds(pl.multiple_of(c * TRAITS, TRAITS), TRAITS)
            p_send[pl.ds(c * per_chunk, per_chunk)] = (
                (p_acc[at] * (1.0 / total_samples))
                .astype(jnp.bfloat16)
                .reshape(per_chunk, kd, width)
            )

        loop(chunks, to_send)

        def p_copy(q):
            return pltpu.make_async_remote_copy(
                src_ref=p_send.at[q],
                dst_ref=p_recv.at[me],
                send_sem=p_ss.at[k, q],
                recv_sem=p_rs.at[k, me],
                device_id=(q, mv),
                device_id_type=MESH,
            )

        each_peer(lambda q: p_copy(q).start())
        p_recv[me] = p_send[me]

        each_peer(lambda q: to_peer(u_all, u_ss.at[k], u_rs.at[k], q).wait_send())

        def t_sent(j):
            @pl.when(mv < nv - 1)
            def _():
                t_copy(k, j, True).wait_send()

            @pl.when(mv > 0)
            def _():
                t_copy(k, j, False).wait_send()

        loop(tiles, t_sent)
        each_peer(lambda q: from_peer(p_recv, p_ss.at[k], p_rs.at[k], q).wait_recv())
        linked = jnp.sum(p_recv[...].astype(jnp.float32), axis=0)
        each_peer(lambda q: p_copy(q).wait_send())

        image = mask_row * linked + RIDGE * direction
        parts = (
            row_sums(residual, residual),
            row_sums(direction, image),
            row_sums(residual, image),
            row_sums(image, image),
        )
        packed = jnp.zeros((kd, LANES), jnp.float32)
        for i, part in enumerate(parts):
            packed = jnp.where(lane == i, part, packed)
        dots[k, mv] = packed

        def dot_copy(slot, peer):
            return pltpu.make_async_remote_copy(
                src_ref=dots.at[k, slot],
                dst_ref=dots.at[k, slot],
                send_sem=dot_ss.at[k, peer],
                recv_sem=dot_rs.at[k, slot],
                device_id=(me, peer),
                device_id_type=MESH,
            )

        def each_block(action):
            loop(nv - 1, lambda i: action(lax.rem(mv + i + 1, nv)))

        each_block(lambda q: dot_copy(mv, q).start())
        each_block(lambda q: dot_copy(q, q).wait_recv())
        all_sums = jnp.sum(dots[k], axis=0)
        norm, product, cross, image_norm = [all_sums[:, i : i + 1] for i in range(4)]
        step = norm / product
        weights = weights + step * direction
        projected = projected + step * linked
        if k + 1 < ITERS:
            residual = residual - step * image
            norm_next = norm - 2.0 * step * cross + step * step * image_norm
            direction = residual + (norm_next / norm) * direction
            u_all[me] = direction
            each_peer(lambda q: to_peer(u_all, u_ss.at[k + 1], u_rs.at[k + 1], q).start())
        each_block(lambda q: dot_copy(mv, q).wait_send())

    sol_ref[...] = weights
    imp_ref[...] = jnp.where(mask_ref[...] == 1, z_ref[...], projected)


def on_device(genotypes, typed_mask, z_scores):
    n, nv = lax.axis_size("samples"), lax.axis_size("vblocks")
    samples_dev, width = genotypes.shape
    kd = z_scores.shape[0]
    traits = n * kd
    tiles = samples_dev // ROWS
    vmem = pl.BlockSpec(memory_space=pltpu.VMEM)
    dma = pltpu.SemaphoreType.DMA
    out = jax.ShapeDtypeStruct((kd, width), jnp.float32)
    return pl.pallas_call(
        functools.partial(kernel, n, nv),
        out_shape=(out, out),
        in_specs=[pl.BlockSpec(memory_space=pl.ANY), vmem, vmem],
        out_specs=(vmem, vmem),
        scratch_shapes=[
            pltpu.VMEM((tiles, ROWS, width), jnp.int32),
            pltpu.VMEM((tiles, ROWS, width), jnp.bfloat16),
            pltpu.VMEM((n, 2 * width // LANES, LANES), jnp.float32),
            pltpu.VMEM((n, kd, width), jnp.float32),
            pltpu.VMEM((tiles, traits, ROWS), jnp.bfloat16),
            pltpu.VMEM((2, tiles, traits, ROWS), jnp.bfloat16),
            pltpu.VMEM((traits, width), jnp.float32),
            pltpu.VMEM((n, kd, width), jnp.bfloat16),
            pltpu.VMEM((n, kd, width), jnp.bfloat16),
            pltpu.VMEM((ITERS, nv, kd, LANES), jnp.float32),
            dma((tiles,)),
            dma((n,)),
            dma((n,)),
            dma((ITERS, n)),
            dma((ITERS, n)),
            dma((ITERS, 2, tiles)),
            dma((ITERS, 2, tiles)),
            dma((ITERS, n)),
            dma((ITERS, n)),
            dma((ITERS, nv)),
            dma((ITERS, nv)),
        ],
        compiler_params=pltpu.CompilerParams(
            collective_id=0, has_side_effects=True, vmem_limit_bytes=56 << 20
        ),
    )(genotypes, typed_mask[None, :], z_scores)


def solution(mesh):
    placed = (P("samples", "vblocks"), P("vblocks"), P("samples", "vblocks"))
    return jax.shard_map(
        on_device,
        mesh=mesh,
        in_specs=placed,
        out_specs=(P("samples", "vblocks"), P("samples", "vblocks")),
        check_vma=False,
    )
```

```python
import functools

import jax
import jax.numpy as jnp
from jax import lax
from jax.experimental import pallas as pl
from jax.experimental.pallas import tpu as pltpu
from jax.sharding import PartitionSpec as P

ITERS = 3
RIDGE = 0.1
EPSILON = 1e-05
MESH = pl.DeviceIdType.MESH
ROWS = 256
TRAITS = 128
LANES = 128


def loop(count, body):
    if count <= 4:
        for index in range(count):
            body(index)
    else:
        lax.fori_loop(0, count, lambda index, carry: (body(index), carry)[1], 0)


def split_high_low(value):
    high = value.astype(jnp.bfloat16)
    low = (value - high.astype(jnp.float32)).astype(jnp.bfloat16)
    return jnp.concatenate([high, low], axis=0)


LEVELS = 32000.0


def decoded_scale(digits):
    return digits[:, 0:1] * jnp.exp2(digits[:, 1:2] - 13.0)


def encode(value):
    rows = value.shape[0]
    biggest = jnp.max(jnp.abs(value), axis=1, keepdims=True)
    wanted = jnp.maximum(biggest, 1e-30) * (1.0 / LEVELS)
    exponent = jnp.floor(jnp.log2(wanted))
    mantissa = jnp.ceil(wanted * jnp.exp2(13.0 - exponent))
    lane = lax.broadcasted_iota(jnp.int32, (rows, LANES), 1)
    digits = jnp.where(lane == 0, mantissa, jnp.where(lane == 1, exponent, 0.0))
    scale = decoded_scale(digits)
    coded = jnp.round(value / scale)
    both = jnp.concatenate([coded, digits], axis=1).astype(jnp.int32).astype(jnp.int16)
    return both, coded * scale


def kernel(
    n,
    nv,
    g_hbm,
    mask_ref,
    z_ref,
    sol_ref,
    imp_ref,
    g_buf,
    x_ref,
    stat,
    u_all,
    t_own,
    t_side,
    p_acc,
    p_send,
    p_pair,
    p_recv,
    dots,
    g_sem,
    stat_ss,
    stat_rs,
    u_ss,
    u_rs,
    t_ss,
    t_rs,
    pair_ss,
    pair_rs,
    p_ss,
    p_rs,
    dot_ss,
    dot_rs,
):
    me = lax.axis_index("samples")
    mv = lax.axis_index("vblocks")
    tiles, _, width = g_buf.shape
    kd = z_ref.shape[0]
    chunks = (n * kd) // TRAITS
    per_chunk = TRAITS // kd
    packs = width // LANES
    total_samples = float(n * tiles * ROWS)

    for c in range(tiles):
        pltpu.make_async_copy(
            g_hbm.at[pl.ds(c * ROWS, ROWS)], g_buf.at[c], g_sem.at[c]
        ).start()

    barrier = pltpu.get_barrier_semaphore()

    def greet_samples(i):
        peer = lax.rem(me + i + 1, n)
        pl.semaphore_signal(barrier, inc=1, device_id=(peer, mv), device_id_type=MESH)

    def greet_blocks(i):
        peer = lax.rem(mv + i + 1, nv)
        pl.semaphore_signal(barrier, inc=1, device_id=(me, peer), device_id_type=MESH)

    loop(n - 1, greet_samples)
    loop(nv - 1, greet_blocks)

    def to_peer(buf, ss, rs, peer):
        return pltpu.make_async_remote_copy(
            src_ref=buf.at[me],
            dst_ref=buf.at[me],
            send_sem=ss.at[peer],
            recv_sem=rs.at[me],
            device_id=(peer, mv),
            device_id_type=MESH,
        )

    def from_peer(buf, ss, rs, peer):
        return pltpu.make_async_remote_copy(
            src_ref=buf.at[peer],
            dst_ref=buf.at[peer],
            send_sem=ss.at[peer],
            recv_sem=rs.at[peer],
            device_id=(peer, mv),
            device_id_type=MESH,
        )

    def each_peer(action):
        loop(n - 1, lambda i: action(lax.rem(me + i + 1, n)))

    mine, parity = me // 2, lax.rem(me, 2)
    partner = me + 1 - 2 * parity
    pairs = n // 2

    def each_far(action):
        loop(pairs - 1, lambda i: action(lax.rem(mine + i + 1, pairs)))

    def far_copy(k, slot, target):
        return pltpu.make_async_remote_copy(
            src_ref=u_all.at[slot],
            dst_ref=u_all.at[slot],
            send_sem=u_ss.at[k, 0, target // 2],
            recv_sem=u_rs.at[k, slot],
            device_id=(target, mv),
            device_id_type=MESH,
        )

    def partner_copy(k, slot):
        return pltpu.make_async_remote_copy(
            src_ref=u_all.at[slot],
            dst_ref=u_all.at[slot],
            send_sem=u_ss.at[k, 1, slot // 2],
            recv_sem=u_rs.at[k, slot],
            device_id=(partner, mv),
            device_id_type=MESH,
        )

    def start_gather(k):
        each_far(lambda f: far_copy(k, me, 2 * f + parity).start())
        partner_copy(k, me).start()

    def end_gather(k):
        def forward(f):
            slot = 2 * f + parity
            far_copy(k, slot, slot).wait_recv()
            partner_copy(k, slot).start()

        each_far(forward)
        loop(pairs, lambda f: partner_copy(k, 2 * f + 1 - parity).wait_recv())

    def gather_sent(k):
        each_far(lambda f: far_copy(k, me, 2 * f + parity).wait_send())
        loop(pairs, lambda f: partner_copy(k, 2 * f + parity).wait_send())

    totals = jnp.zeros((1, width), jnp.float32)
    squares = jnp.zeros((1, width), jnp.float32)
    for c in range(tiles):
        pltpu.make_async_copy(
            g_hbm.at[pl.ds(c * ROWS, ROWS)], g_buf.at[c], g_sem.at[c]
        ).wait()
        dosage = g_buf[c].astype(jnp.float32)
        totals = totals + jnp.sum(dosage, axis=0, keepdims=True)
        squares = squares + jnp.sum(dosage * dosage, axis=0, keepdims=True)
    for i in range(packs):
        stat[me, i : i + 1, :] = totals[:, i * LANES : (i + 1) * LANES]
        stat[me, packs + i : packs + i + 1, :] = squares[:, i * LANES : (i + 1) * LANES]
    mask_row = mask_ref[...].astype(jnp.float32)
    residual = mask_row * z_ref[...]
    u_all[me], direction = encode(residual)

    pl.semaphore_wait(barrier, n - 1 + nv - 1)
    each_peer(lambda q: to_peer(stat, stat_ss, stat_rs, q).start())
    start_gather(0)
    each_peer(lambda q: from_peer(stat, stat_ss, stat_rs, q).wait_recv())
    summed = jnp.sum(stat[...], axis=0)
    totals = jnp.concatenate([summed[i : i + 1] for i in range(packs)], axis=1)
    squares = jnp.concatenate([summed[packs + i : packs + i + 1] for i in range(packs)], axis=1)
    mean_dosage = totals / total_samples
    variance = squares / total_samples - mean_dosage * mean_dosage
    scale = lax.rsqrt(variance + EPSILON)
    for c in range(tiles):
        dosage = g_buf[c].astype(jnp.float32)
        x_ref[c] = ((dosage - mean_dosage) * scale).astype(jnp.bfloat16)
    each_peer(lambda q: to_peer(stat, stat_ss, stat_rs, q).wait_send())

    def t_copy(k, j, ahead):
        side = 0 if ahead else 1
        return pltpu.make_async_remote_copy(
            src_ref=t_own.at[j],
            dst_ref=t_side.at[side, j],
            send_sem=t_ss.at[k, side, j],
            recv_sem=t_rs.at[k, side, j],
            device_id=(me, mv + 1 if ahead else mv - 1),
            device_id_type=MESH,
        )

    @pl.when(mv == 0)
    def _():
        t_side[0] = jnp.zeros(t_side.shape[1:], t_side.dtype)

    @pl.when(mv == nv - 1)
    def _():
        t_side[1] = jnp.zeros(t_side.shape[1:], t_side.dtype)

    lane = lax.broadcasted_iota(jnp.int32, (kd, LANES), 1)

    def row_sums(first, second):
        return jnp.sum(first * second, axis=1, keepdims=True)

    weights = jnp.zeros_like(residual)
    projected = jnp.zeros_like(residual)
    for k in range(ITERS):
        end_gather(k)

        def products(j):
            def one(c):
                coded = u_all[pl.ds(c * per_chunk, per_chunk)].astype(jnp.int32)
                coded = coded.astype(jnp.float32).reshape(TRAITS, width + LANES)
                both = lax.dot_general(
                    split_high_low(coded[:, :width]),
                    x_ref[j],
                    (((1,), (1,)), ((), ())),
                    preferred_element_type=jnp.float32,
                )
                t_own[j, pl.ds(pl.multiple_of(c * TRAITS, TRAITS), TRAITS)] = (
                    (both[:TRAITS] + both[TRAITS:]) * decoded_scale(coded[:, width:])
                ).astype(jnp.bfloat16)

            loop(chunks, one)

            @pl.when(mv < nv - 1)
            def _():
                t_copy(k, j, True).start()

            @pl.when(mv > 0)
            def _():
                t_copy(k, j, False).start()

        loop(tiles, products)

        def back(j):
            @pl.when(mv > 0)
            def _():
                t_copy(k, j, True).wait_recv()

            @pl.when(mv < nv - 1)
            def _():
                t_copy(k, j, False).wait_recv()

            def one(c):
                at = pl.ds(pl.multiple_of(c * TRAITS, TRAITS), TRAITS)
                mixed = t_own[j, at].astype(jnp.float32) + 0.5 * (
                    t_side[0, j, at].astype(jnp.float32) + t_side[1, j, at].astype(jnp.float32)
                )
                part = jnp.dot(
                    mixed.astype(jnp.bfloat16), x_ref[j], preferred_element_type=jnp.float32
                )
                if isinstance(j, int) and j == 0:
                    p_acc[at] = part
                else:
                    p_acc[at] = p_acc[at] + part

            loop(chunks, one)

        if tiles > 4:
            p_acc[...] = jnp.zeros_like(p_acc)
        loop(tiles, back)

        def to_send(c):
            at = pl.ds(pl.multiple_of(c * TRAITS, TRAITS), TRAITS)
            p_send[pl.ds(c * per_chunk, per_chunk)] = (
                (p_acc[at] * (1.0 / total_samples))
                .astype(jnp.bfloat16)
                .reshape(per_chunk, kd, width)
            )

        loop(chunks, to_send)

        def pair_copy(f, own):
            slot = 2 * f + (parity if own else 1 - parity)
            return pltpu.make_async_remote_copy(
                src_ref=p_send.at[slot],
                dst_ref=p_pair.at[f],
                send_sem=pair_ss.at[k, f],
                recv_sem=pair_rs.at[k, f],
                device_id=(partner, mv),
                device_id_type=MESH,
            )

        def p_copy(f, slot):
            return pltpu.make_async_remote_copy(
                src_ref=p_send.at[2 * f + parity],
                dst_ref=p_recv.at[slot],
                send_sem=p_ss.at[k, f],
                recv_sem=p_rs.at[k, slot],
                device_id=(2 * f + parity, mv),
                device_id_type=MESH,
            )

        def add_pair(f):
            pair_copy(f, True).wait_recv()
            slot = 2 * f + parity
            p_send[slot] = (
                p_send[slot].astype(jnp.float32) + p_pair[f].astype(jnp.float32)
            ).astype(jnp.bfloat16)

        def add_and_send(f):
            add_pair(f)
            p_copy(f, mine).start()

        gather_sent(k)
        each_far(lambda f: pair_copy(f, False).start())
        pair_copy(mine, False).start()
        each_far(add_and_send)
        add_pair(mine)
        p_recv[mine] = p_send[me]


        def t_sent(j):
            @pl.when(mv < nv - 1)
            def _():
                t_copy(k, j, True).wait_send()

            @pl.when(mv > 0)
            def _():
                t_copy(k, j, False).wait_send()

        loop(tiles, t_sent)
        each_far(lambda f: p_copy(f, f).wait_recv())
        linked = jnp.sum(p_recv[...].astype(jnp.float32), axis=0)
        loop(pairs, lambda f: pair_copy(f, False).wait_send())
        each_far(lambda f: p_copy(f, mine).wait_send())

        image = mask_row * linked + RIDGE * direction
        parts = (
            row_sums(residual, residual),
            row_sums(direction, image),
            row_sums(residual, image),
            row_sums(image, image),
        )
        packed = jnp.zeros((kd, LANES), jnp.float32)
        for i, part in enumerate(parts):
            packed = jnp.where(lane == i, part, packed)
        dots[k, mv] = packed

        def dot_copy(slot, peer):
            return pltpu.make_async_remote_copy(
                src_ref=dots.at[k, slot],
                dst_ref=dots.at[k, slot],
                send_sem=dot_ss.at[k, peer],
                recv_sem=dot_rs.at[k, slot],
                device_id=(me, peer),
                device_id_type=MESH,
            )

        def each_block(action):
            loop(nv - 1, lambda i: action(lax.rem(mv + i + 1, nv)))

        each_block(lambda q: dot_copy(mv, q).start())
        each_block(lambda q: dot_copy(q, q).wait_recv())
        all_sums = jnp.sum(dots[k], axis=0)
        norm, product, cross, image_norm = [all_sums[:, i : i + 1] for i in range(4)]
        step = norm / product
        weights = weights + step * direction
        projected = projected + step * linked
        if k + 1 < ITERS:
            residual = residual - step * image
            norm_next = norm - 2.0 * step * cross + step * step * image_norm
            direction = residual + (norm_next / norm) * direction
            u_all[me], direction = encode(direction)
            start_gather(k + 1)
        each_block(lambda q: dot_copy(mv, q).wait_send())

    sol_ref[...] = weights
    imp_ref[...] = jnp.where(mask_ref[...] == 1, z_ref[...], projected)


def on_device(genotypes, typed_mask, z_scores):
    n, nv = lax.axis_size("samples"), lax.axis_size("vblocks")
    samples_dev, width = genotypes.shape
    kd = z_scores.shape[0]
    traits = n * kd
    tiles = samples_dev // ROWS
    vmem = pl.BlockSpec(memory_space=pltpu.VMEM)
    dma = pltpu.SemaphoreType.DMA
    out = jax.ShapeDtypeStruct((kd, width), jnp.float32)
    return pl.pallas_call(
        functools.partial(kernel, n, nv),
        out_shape=(out, out),
        in_specs=[pl.BlockSpec(memory_space=pl.ANY), vmem, vmem],
        out_specs=(vmem, vmem),
        scratch_shapes=[
            pltpu.VMEM((tiles, ROWS, width), jnp.int32),
            pltpu.VMEM((tiles, ROWS, width), jnp.bfloat16),
            pltpu.VMEM((n, 2 * width // LANES, LANES), jnp.float32),
            pltpu.VMEM((n, kd, width + LANES), jnp.int16),
            pltpu.VMEM((tiles, traits, ROWS), jnp.bfloat16),
            pltpu.VMEM((2, tiles, traits, ROWS), jnp.bfloat16),
            pltpu.VMEM((traits, width), jnp.float32),
            pltpu.VMEM((n, kd, width), jnp.bfloat16),
            pltpu.VMEM((n // 2, kd, width), jnp.bfloat16),
            pltpu.VMEM((n // 2, kd, width), jnp.bfloat16),
            pltpu.VMEM((ITERS, nv, kd, LANES), jnp.float32),
            dma((tiles,)),
            dma((n,)),
            dma((n,)),
            dma((ITERS, 2, n // 2)),
            dma((ITERS, n)),
            dma((ITERS, 2, tiles)),
            dma((ITERS, 2, tiles)),
            dma((ITERS, n // 2)),
            dma((ITERS, n // 2)),
            dma((ITERS, n // 2)),
            dma((ITERS, n // 2)),
            dma((ITERS, nv)),
            dma((ITERS, nv)),
        ],
        compiler_params=pltpu.CompilerParams(
            collective_id=0, has_side_effects=True, vmem_limit_bytes=56 << 20
        ),
    )(genotypes, typed_mask[None, :], z_scores)


def solution(mesh):
    placed = (P("samples", "vblocks"), P("vblocks"), P("samples", "vblocks"))
    return jax.shard_map(
        on_device,
        mesh=mesh,
        in_specs=placed,
        out_specs=(P("samples", "vblocks"), P("samples", "vblocks")),
        check_vma=False,
    )
```

```python
import functools

import jax
import jax.numpy as jnp
from jax import lax
from jax.experimental import pallas as pl
from jax.experimental.pallas import tpu as pltpu
from jax.sharding import PartitionSpec as P

ITERS = 3
RIDGE = 0.1
EPSILON = 1e-05
MESH = pl.DeviceIdType.MESH
ROWS = 256
TRAITS = 128
GROUPS = 1
LANES = 128


def loop(count, body):
    if count <= 4:
        for index in range(count):
            body(index)
    else:
        lax.fori_loop(0, count, lambda index, carry: (body(index), carry)[1], 0)


def split_high_low(value):
    high = value.astype(jnp.bfloat16)
    low = (value - high.astype(jnp.float32)).astype(jnp.bfloat16)
    return jnp.concatenate([high, low], axis=0)


LEVELS = 32000.0


def decoded_scale(digits):
    return digits[:, 0:1] * jnp.exp2(digits[:, 1:2] - 13.0)


def encode(value):
    rows = value.shape[0]
    biggest = jnp.max(jnp.abs(value), axis=1, keepdims=True)
    wanted = jnp.maximum(biggest, 1e-30) * (1.0 / LEVELS)
    exponent = jnp.floor(jnp.log2(wanted))
    mantissa = jnp.ceil(wanted * jnp.exp2(13.0 - exponent))
    lane = lax.broadcasted_iota(jnp.int32, (rows, LANES), 1)
    digits = jnp.where(lane == 0, mantissa, jnp.where(lane == 1, exponent, 0.0))
    scale = decoded_scale(digits)
    coded = jnp.round(value / scale)
    both = jnp.concatenate([coded, digits], axis=1).astype(jnp.int32).astype(jnp.int16)
    return both, coded * scale


def kernel(
    n,
    nv,
    g_hbm,
    mask_ref,
    z_ref,
    sol_ref,
    imp_ref,
    g_buf,
    x_ref,
    xt_ref,
    stat,
    u_all,
    u_hl,
    u_scale,
    res_ref,
    dir_ref,
    link_ref,
    t_own,
    t_side,
    p_acc,
    p_send,
    p_pair,
    p_recv,
    dots,
    g_sem,
    stat_ss,
    stat_rs,
    u_ss,
    u_rs,
    t_ss,
    t_rs,
    pair_ss,
    pair_rs,
    p_ss,
    p_rs,
    dot_ss,
    dot_rs,
):
    me = lax.axis_index("samples")
    mv = lax.axis_index("vblocks")
    tiles, _, width = g_buf.shape
    kd = z_ref.shape[0]
    packs = width // LANES
    total_samples = float(n * tiles * ROWS)

    for c in range(tiles):
        pltpu.make_async_copy(
            g_hbm.at[pl.ds(c * ROWS, ROWS)], g_buf.at[c], g_sem.at[c]
        ).start()

    barrier = pltpu.get_barrier_semaphore()

    def greet_samples(i):
        peer = lax.rem(me + i + 1, n)
        pl.semaphore_signal(barrier, inc=1, device_id=(peer, mv), device_id_type=MESH)

    def greet_blocks(i):
        peer = lax.rem(mv + i + 1, nv)
        pl.semaphore_signal(barrier, inc=1, device_id=(me, peer), device_id_type=MESH)

    loop(n - 1, greet_samples)
    loop(nv - 1, greet_blocks)

    def to_peer(buf, ss, rs, peer):
        return pltpu.make_async_remote_copy(
            src_ref=buf.at[me],
            dst_ref=buf.at[me],
            send_sem=ss.at[peer],
            recv_sem=rs.at[me],
            device_id=(peer, mv),
            device_id_type=MESH,
        )

    def from_peer(buf, ss, rs, peer):
        return pltpu.make_async_remote_copy(
            src_ref=buf.at[peer],
            dst_ref=buf.at[peer],
            send_sem=ss.at[peer],
            recv_sem=rs.at[peer],
            device_id=(peer, mv),
            device_id_type=MESH,
        )

    def each_peer(action):
        loop(n - 1, lambda i: action(lax.rem(me + i + 1, n)))

    mine, parity = me // 2, lax.rem(me, 2)
    partner = me + 1 - 2 * parity
    pairs = n // 2
    my_group = lax.rem(mine, GROUPS)
    members = pairs // GROUPS

    def each_far(action):
        loop(pairs - 1, lambda i: action(lax.rem(mine + i + 1, pairs)))

    def each_member(g, action):
        start = mine // GROUPS + 1
        loop(members, lambda i: action(GROUPS * lax.rem(start + i, members) + g))

    def slot_of(ref, f, side):
        return ref.at[lax.rem(f, GROUPS), 2 * (f // GROUPS) + side]

    def far_copy(k, f, target):
        return pltpu.make_async_remote_copy(
            src_ref=slot_of(u_all, f, parity),
            dst_ref=slot_of(u_all, f, parity),
            send_sem=u_ss.at[k, 0, target],
            recv_sem=u_rs.at[k, 2 * f + parity],
            device_id=(2 * target + parity, mv),
            device_id_type=MESH,
        )

    def partner_copy(k, f, side):
        return pltpu.make_async_remote_copy(
            src_ref=slot_of(u_all, f, side),
            dst_ref=slot_of(u_all, f, side),
            send_sem=u_ss.at[k, 1, f],
            recv_sem=u_rs.at[k, 2 * f + side],
            device_id=(partner, mv),
            device_id_type=MESH,
        )

    def start_gather(k):
        each_far(lambda f: far_copy(k, mine, f).start())
        partner_copy(k, mine, parity).start()

    def end_gather(k, g):
        def forward(f):
            @pl.when(f != mine)
            def _():
                far_copy(k, f, f).wait_recv()
                partner_copy(k, f, parity).start()

        each_member(g, forward)
        each_member(g, lambda f: partner_copy(k, f, 1 - parity).wait_recv())

    def gather_sent(k, g):
        @pl.when(my_group == g)
        def _():
            each_far(lambda f: far_copy(k, mine, f).wait_send())

        each_member(g, lambda f: partner_copy(k, f, parity).wait_send())

    totals = jnp.zeros((1, width), jnp.float32)
    squares = jnp.zeros((1, width), jnp.float32)
    for c in range(tiles):
        pltpu.make_async_copy(
            g_hbm.at[pl.ds(c * ROWS, ROWS)], g_buf.at[c], g_sem.at[c]
        ).wait()
        dosage = g_buf[c].astype(jnp.float32)
        totals = totals + jnp.sum(dosage, axis=0, keepdims=True)
        squares = squares + jnp.sum(dosage * dosage, axis=0, keepdims=True)
    for i in range(packs):
        stat[me, i : i + 1, :] = totals[:, i * LANES : (i + 1) * LANES]
        stat[me, packs + i : packs + i + 1, :] = squares[:, i * LANES : (i + 1) * LANES]
    mask_row = mask_ref[...].astype(jnp.float32)
    residual = mask_row * z_ref[...]
    res_ref[...] = residual
    my_slot = slot_of(u_all, mine, parity)
    my_slot[...], dir_ref[...] = encode(residual)
    sol_ref[...] = jnp.zeros_like(residual)
    imp_ref[...] = jnp.zeros_like(residual)

    pl.semaphore_wait(barrier, n - 1 + nv - 1)
    each_peer(lambda q: to_peer(stat, stat_ss, stat_rs, q).start())
    start_gather(0)
    each_peer(lambda q: from_peer(stat, stat_ss, stat_rs, q).wait_recv())
    summed = jnp.sum(stat[...], axis=0)
    totals = jnp.concatenate([summed[i : i + 1] for i in range(packs)], axis=1)
    squares = jnp.concatenate([summed[packs + i : packs + i + 1] for i in range(packs)], axis=1)
    mean_dosage = totals / total_samples
    variance = squares / total_samples - mean_dosage * mean_dosage
    scale = lax.rsqrt(variance + EPSILON)
    for c in range(tiles):
        dosage = g_buf[c].astype(jnp.float32)
        x_ref[c] = ((dosage - mean_dosage) * scale).astype(jnp.bfloat16)
    each_peer(lambda q: to_peer(stat, stat_ss, stat_rs, q).wait_send())

    def t_copy(k, g, j, ahead):
        side = 0 if ahead else 1
        return pltpu.make_async_remote_copy(
            src_ref=t_own.at[g, j],
            dst_ref=t_side.at[g, side, j],
            send_sem=t_ss.at[k, g, side, j],
            recv_sem=t_rs.at[k, g, side, j],
            device_id=(me, mv + 1 if ahead else mv - 1),
            device_id_type=MESH,
        )

    @pl.when(mv == 0)
    def _():
        for g in range(GROUPS):
            t_side[g, 0] = jnp.zeros(t_side.shape[2:], t_side.dtype)

    @pl.when(mv == nv - 1)
    def _():
        for g in range(GROUPS):
            t_side[g, 1] = jnp.zeros(t_side.shape[2:], t_side.dtype)

    lane = lax.broadcasted_iota(jnp.int32, (kd, LANES), 1)

    def row_sums(first, second):
        return jnp.sum(first * second, axis=1, keepdims=True)

    traits = u_hl.shape[1] // 2
    chunks = u_hl.shape[0]
    per_chunk = traits // kd

    def rows_at(c):
        return pl.ds(pl.multiple_of(c * traits, traits), traits)

    def project(k, g):
        end_gather(k, g)

        def decode(c):
            coded = u_all[g, pl.ds(c * per_chunk, per_chunk)].astype(jnp.int32)
            coded = coded.astype(jnp.float32).reshape(traits, width + LANES)
            u_hl[c] = split_high_low(coded[:, :width])
            u_scale[c] = jnp.broadcast_to(decoded_scale(coded[:, width:]), (traits, LANES))

        loop(chunks, decode)

        def products(j):
            def one(c):
                if k == 0:
                    both = lax.dot_general(
                        u_hl[c],
                        x_ref[j],
                        (((1,), (1,)), ((), ())),
                        preferred_element_type=jnp.float32,
                    )
                else:
                    both = jnp.dot(u_hl[c], xt_ref[j], preferred_element_type=jnp.float32)
                t_own[g, j, rows_at(c)] = (
                    (both[:traits] + both[traits:]) * u_scale[c, :, 0:1]
                ).astype(jnp.bfloat16)

            loop(chunks, one)

            @pl.when(mv < nv - 1)
            def _():
                t_copy(k, g, j, True).start()

            @pl.when(mv > 0)
            def _():
                t_copy(k, g, j, False).start()

        loop(tiles, products)

    def pair_copy(k, f, side):
        return pltpu.make_async_remote_copy(
            src_ref=slot_of(p_send, f, side),
            dst_ref=p_pair.at[f],
            send_sem=pair_ss.at[k, f],
            recv_sem=pair_rs.at[k, f],
            device_id=(partner, mv),
            device_id_type=MESH,
        )

    def p_copy(k, f, place):
        return pltpu.make_async_remote_copy(
            src_ref=slot_of(p_send, f, parity),
            dst_ref=p_recv.at[place],
            send_sem=p_ss.at[k, f],
            recv_sem=p_rs.at[k, place],
            device_id=(2 * f + parity, mv),
            device_id_type=MESH,
        )

    def project_back(k, g):
        def back(j):
            @pl.when(mv > 0)
            def _():
                t_copy(k, g, j, True).wait_recv()

            @pl.when(mv < nv - 1)
            def _():
                t_copy(k, g, j, False).wait_recv()

            def one(c):
                at = rows_at(c)
                sides = t_side[g, 0, j, at].astype(jnp.float32) + t_side[g, 1, j, at].astype(
                    jnp.float32
                )
                mixed = t_own[g, j, at].astype(jnp.float32) + 0.5 * sides
                part = jnp.dot(
                    mixed.astype(jnp.bfloat16), x_ref[j], preferred_element_type=jnp.float32
                )
                if isinstance(j, int) and j == 0:
                    p_acc[at] = part
                else:
                    p_acc[at] = p_acc[at] + part

            loop(chunks, one)

        if tiles > 4:
            p_acc[...] = jnp.zeros_like(p_acc)
        loop(tiles, back)

        def to_send(c):
            p_send[g, pl.ds(c * per_chunk, per_chunk)] = (
                (p_acc[rows_at(c)] * (1.0 / total_samples))
                .astype(jnp.bfloat16)
                .reshape(per_chunk, kd, width)
            )

        loop(chunks, to_send)
        gather_sent(k, g)
        each_member(g, lambda f: pair_copy(k, f, 1 - parity).start())

        def t_sent(j):
            @pl.when(mv < nv - 1)
            def _():
                t_copy(k, g, j, True).wait_send()

            @pl.when(mv > 0)
            def _():
                t_copy(k, g, j, False).wait_send()

        loop(tiles, t_sent)

    def add_pairs(k, g):
        def add(f):
            pair_copy(k, f, parity).wait_recv()
            held = slot_of(p_send, f, parity)
            both = held[...].astype(jnp.float32) + p_pair[f].astype(jnp.float32)
            held[...] = both.astype(jnp.bfloat16)

            @pl.when(f != mine)
            def _():
                p_copy(k, f, mine).start()

            @pl.when(f == mine)
            def _():
                p_recv[mine] = held[...]

        each_member(g, add)

    def dot_copy(k, slot, peer):
        return pltpu.make_async_remote_copy(
            src_ref=dots.at[k, slot],
            dst_ref=dots.at[k, slot],
            send_sem=dot_ss.at[k, peer],
            recv_sem=dot_rs.at[k, slot],
            device_id=(me, peer),
            device_id_type=MESH,
        )

    def each_block(action):
        loop(nv - 1, lambda i: action(lax.rem(mv + i + 1, nv)))

    def send_dots(k):
        each_far(lambda f: p_copy(k, f, f).wait_recv())
        linked = jnp.sum(p_recv[...].astype(jnp.float32), axis=0)
        residual, direction = res_ref[...], dir_ref[...]
        image = mask_row * linked + RIDGE * direction
        link_ref[...] = linked
        parts = (
            row_sums(residual, residual),
            row_sums(direction, image),
            row_sums(residual, image),
            row_sums(image, image),
        )
        packed = jnp.zeros((kd, LANES), jnp.float32)
        for i, part in enumerate(parts):
            packed = jnp.where(lane == i, part, packed)
        dots[k, mv] = packed
        each_block(lambda q: dot_copy(k, mv, q).start())

    def update(k):
        each_block(lambda q: dot_copy(k, q, q).wait_recv())
        all_sums = jnp.sum(dots[k], axis=0)
        norm, product, cross, image_norm = [all_sums[:, i : i + 1] for i in range(4)]
        step = norm / product
        direction, linked = dir_ref[...], link_ref[...]
        if k + 1 < ITERS:
            image = mask_row * linked + RIDGE * direction
            residual = res_ref[...] - step * image
            norm_next = norm - 2.0 * step * cross + step * step * image_norm
            my_slot[...], dir_ref[...] = encode(residual + (norm_next / norm) * direction)
            start_gather(k + 1)
            res_ref[...] = residual
            sol_ref[...] = sol_ref[...] + step * direction
            imp_ref[...] = imp_ref[...] + step * linked
        else:
            sol_ref[...] = sol_ref[...] + step * direction
            projected = imp_ref[...] + step * linked
            imp_ref[...] = jnp.where(mask_ref[...] == 1, z_ref[...], projected)

    def finish(k, g):
        each_member(g, lambda f: pair_copy(k, f, 1 - parity).wait_send())

        def sent(f):
            @pl.when(f != mine)
            def _():
                p_copy(k, f, mine).wait_send()

        each_member(g, sent)

        @pl.when(my_group == g)
        def _():
            each_block(lambda q: dot_copy(k, mv, q).wait_send())

    def transpose(j):
        xt_ref[j] = x_ref[j].T

    groups = range(GROUPS)
    for k in range(ITERS):
        for g in groups:
            project(k, g)
        for g in groups:
            project_back(k, g)
        if k == 0:
            loop(tiles // 2, transpose)
        for g in groups:
            add_pairs(k, g)
        if k == 0:
            loop(tiles - tiles // 2, lambda j: transpose(tiles // 2 + j))
        for g in groups:
            pl.when(my_group == g)(functools.partial(send_dots, k))
        for g in groups:
            pl.when(my_group == g)(functools.partial(update, k))
        for g in groups:
            finish(k, g)


def on_device(genotypes, typed_mask, z_scores):
    n, nv = lax.axis_size("samples"), lax.axis_size("vblocks")
    samples_dev, width = genotypes.shape
    kd = z_scores.shape[0]
    group_traits = n * kd // GROUPS
    tiles = samples_dev // ROWS
    vmem = pl.BlockSpec(memory_space=pltpu.VMEM)
    dma = pltpu.SemaphoreType.DMA
    out = jax.ShapeDtypeStruct((kd, width), jnp.float32)
    return pl.pallas_call(
        functools.partial(kernel, n, nv),
        out_shape=(out, out),
        in_specs=[pl.BlockSpec(memory_space=pl.ANY), vmem, vmem],
        out_specs=(vmem, vmem),
        scratch_shapes=[
            pltpu.VMEM((tiles, ROWS, width), jnp.int32),
            pltpu.VMEM((tiles, ROWS, width), jnp.bfloat16),
            pltpu.VMEM((tiles, width, ROWS), jnp.bfloat16),
            pltpu.VMEM((n, 2 * width // LANES, LANES), jnp.float32),
            pltpu.VMEM((GROUPS, n // GROUPS, kd, width + LANES), jnp.int16),
            pltpu.VMEM((group_traits // TRAITS, 2 * TRAITS, width), jnp.bfloat16),
            pltpu.VMEM((group_traits // TRAITS, TRAITS, LANES), jnp.float32),
            pltpu.VMEM((kd, width), jnp.float32),
            pltpu.VMEM((kd, width), jnp.float32),
            pltpu.VMEM((kd, width), jnp.float32),
            pltpu.VMEM((GROUPS, tiles, group_traits, ROWS), jnp.bfloat16),
            pltpu.VMEM((GROUPS, 2, tiles, group_traits, ROWS), jnp.bfloat16),
            pltpu.VMEM((group_traits, width), jnp.float32),
            pltpu.VMEM((GROUPS, n // GROUPS, kd, width), jnp.bfloat16),
            pltpu.VMEM((n // 2, kd, width), jnp.bfloat16),
            pltpu.VMEM((n // 2, kd, width), jnp.bfloat16),
            pltpu.VMEM((ITERS, nv, kd, LANES), jnp.float32),
            dma((tiles,)),
            dma((n,)),
            dma((n,)),
            dma((ITERS, 2, n // 2)),
            dma((ITERS, n)),
            dma((ITERS, GROUPS, 2, tiles)),
            dma((ITERS, GROUPS, 2, tiles)),
            dma((ITERS, n // 2)),
            dma((ITERS, n // 2)),
            dma((ITERS, n // 2)),
            dma((ITERS, n // 2)),
            dma((ITERS, nv)),
            dma((ITERS, nv)),
        ],
        compiler_params=pltpu.CompilerParams(
            collective_id=0, has_side_effects=True, vmem_limit_bytes=56 << 20
        ),
    )(genotypes, typed_mask[None, :], z_scores)


def solution(mesh):
    placed = (P("samples", "vblocks"), P("vblocks"), P("samples", "vblocks"))
    return jax.shard_map(
        on_device,
        mesh=mesh,
        in_specs=placed,
        out_specs=(P("samples", "vblocks"), P("samples", "vblocks")),
        check_vma=False,
    )
```

```python
import functools

import jax
import jax.numpy as jnp
from jax import lax
from jax.experimental import pallas as pl
from jax.experimental.pallas import tpu as pltpu
from jax.sharding import PartitionSpec as P

ITERS = 3
RIDGE = 0.1
EPSILON = 1e-05
MESH = pl.DeviceIdType.MESH
ROWS = 256
TRAITS = 128
GROUPS = 1
LANES = 128


def loop(count, body):
    if count <= 4:
        for index in range(count):
            body(index)
    else:
        lax.fori_loop(0, count, lambda index, carry: (body(index), carry)[1], 0)


def split_high_low(value):
    high = value.astype(jnp.bfloat16)
    low = (value - high.astype(jnp.float32)).astype(jnp.bfloat16)
    return jnp.concatenate([high, low], axis=0)


LEVELS = 32000.0


def decoded_scale(digits):
    return digits[:, 0:1] * jnp.exp2(digits[:, 1:2] - 13.0)


def encode(value):
    rows = value.shape[0]
    biggest = jnp.max(jnp.abs(value), axis=1, keepdims=True)
    wanted = jnp.maximum(biggest, 1e-28) * (1.0 / LEVELS)
    exponent = jnp.floor(jnp.log2(wanted))
    mantissa = jnp.ceil(wanted * jnp.exp2(13.0 - exponent))
    lane = lax.broadcasted_iota(jnp.int32, (rows, LANES), 1)
    digits = jnp.where(lane == 0, mantissa, jnp.where(lane == 1, exponent, 0.0))
    scale = decoded_scale(digits)
    coded = jnp.round(value * (1.0 / scale))
    both = jnp.concatenate([coded, digits], axis=1).astype(jnp.int32).astype(jnp.int16)
    return both, coded * scale


def decode_rows(both):
    both = both.astype(jnp.int32).astype(jnp.float32)
    width = both.shape[1] - LANES
    return both[:, :width] * decoded_scale(both[:, width:])


def kernel(
    n,
    nv,
    g_hbm,
    mask_ref,
    z_ref,
    sol_ref,
    imp_ref,
    g_buf,
    x_ref,
    xt_ref,
    stat,
    u_all,
    u_hl,
    u_scale,
    res_ref,
    dir_ref,
    link_ref,
    t_own,
    t_side,
    p_acc,
    p_send,
    p_pair,
    p_recv,
    norms,
    block_forms,
    sample_forms,
    g_sem,
    stat_ss,
    stat_rs,
    u_ss,
    u_rs,
    t_ss,
    t_rs,
    pair_ss,
    pair_rs,
    p_ss,
    p_rs,
    norm_ss,
    norm_rs,
    bf_ss,
    bf_rs,
    sf_ss,
    sf_rs,
):
    me = lax.axis_index("samples")
    mv = lax.axis_index("vblocks")
    tiles, _, width = g_buf.shape
    kd = z_ref.shape[0]
    packs = width // LANES
    total_samples = float(n * tiles * ROWS)

    for c in range(tiles):
        pltpu.make_async_copy(
            g_hbm.at[pl.ds(c * ROWS, ROWS)], g_buf.at[c], g_sem.at[c]
        ).start()

    barrier = pltpu.get_barrier_semaphore()

    def greet_samples(i):
        peer = lax.rem(me + i + 1, n)
        pl.semaphore_signal(barrier, inc=1, device_id=(peer, mv), device_id_type=MESH)

    def greet_blocks(i):
        peer = lax.rem(mv + i + 1, nv)
        pl.semaphore_signal(barrier, inc=1, device_id=(me, peer), device_id_type=MESH)

    loop(n - 1, greet_samples)
    loop(nv - 1, greet_blocks)

    def to_peer(buf, ss, rs, peer):
        return pltpu.make_async_remote_copy(
            src_ref=buf.at[me],
            dst_ref=buf.at[me],
            send_sem=ss.at[peer],
            recv_sem=rs.at[me],
            device_id=(peer, mv),
            device_id_type=MESH,
        )

    def from_peer(buf, ss, rs, peer):
        return pltpu.make_async_remote_copy(
            src_ref=buf.at[peer],
            dst_ref=buf.at[peer],
            send_sem=ss.at[peer],
            recv_sem=rs.at[peer],
            device_id=(peer, mv),
            device_id_type=MESH,
        )

    def each_peer(action):
        loop(n - 1, lambda i: action(lax.rem(me + i + 1, n)))

    mine, parity = me // 2, lax.rem(me, 2)
    partner = me + 1 - 2 * parity
    pairs = n // 2
    my_group = lax.rem(mine, GROUPS)
    members = pairs // GROUPS

    def each_far(action):
        loop(pairs - 1, lambda i: action(lax.rem(mine + i + 1, pairs)))

    def each_member(g, action):
        start = mine // GROUPS + 1
        loop(members, lambda i: action(GROUPS * lax.rem(start + i, members) + g))

    def slot_of(ref, f, side):
        return ref.at[lax.rem(f, GROUPS), 2 * (f // GROUPS) + side]

    def far_copy(k, f, target):
        return pltpu.make_async_remote_copy(
            src_ref=slot_of(u_all, f, parity),
            dst_ref=slot_of(u_all, f, parity),
            send_sem=u_ss.at[k, 0, target],
            recv_sem=u_rs.at[k, 2 * f + parity],
            device_id=(2 * target + parity, mv),
            device_id_type=MESH,
        )

    def partner_copy(k, f, side):
        return pltpu.make_async_remote_copy(
            src_ref=slot_of(u_all, f, side),
            dst_ref=slot_of(u_all, f, side),
            send_sem=u_ss.at[k, 1, f],
            recv_sem=u_rs.at[k, 2 * f + side],
            device_id=(partner, mv),
            device_id_type=MESH,
        )

    def start_gather(k):
        each_far(lambda f: far_copy(k, mine, f).start())
        partner_copy(k, mine, parity).start()

    def end_gather(k, g):
        def forward(f):
            @pl.when(f != mine)
            def _():
                far_copy(k, f, f).wait_recv()
                partner_copy(k, f, parity).start()

        each_member(g, forward)
        each_member(g, lambda f: partner_copy(k, f, 1 - parity).wait_recv())

    def gather_sent(k, g):
        @pl.when(my_group == g)
        def _():
            each_far(lambda f: far_copy(k, mine, f).wait_send())

        each_member(g, lambda f: partner_copy(k, f, parity).wait_send())

    totals = jnp.zeros((1, width), jnp.float32)
    squares = jnp.zeros((1, width), jnp.float32)
    for c in range(tiles):
        pltpu.make_async_copy(
            g_hbm.at[pl.ds(c * ROWS, ROWS)], g_buf.at[c], g_sem.at[c]
        ).wait()
        dosage = g_buf[c].astype(jnp.float32)
        totals = totals + jnp.sum(dosage, axis=0, keepdims=True)
        squares = squares + jnp.sum(dosage * dosage, axis=0, keepdims=True)
    for i in range(packs):
        stat[me, i : i + 1, :] = totals[:, i * LANES : (i + 1) * LANES]
        stat[me, packs + i : packs + i + 1, :] = squares[:, i * LANES : (i + 1) * LANES]
    mask_row = mask_ref[...].astype(jnp.float32)
    residual = mask_row * z_ref[...]
    my_slot = slot_of(u_all, mine, parity)
    my_slot[...], res_ref[...] = encode(residual)
    dir_ref[...] = jnp.zeros_like(residual)
    link_ref[...] = jnp.zeros_like(residual)
    sol_ref[...] = jnp.zeros_like(residual)
    imp_ref[...] = jnp.zeros_like(residual)

    pl.semaphore_wait(barrier, n - 1 + nv - 1)
    each_peer(lambda q: to_peer(stat, stat_ss, stat_rs, q).start())
    start_gather(0)
    each_peer(lambda q: from_peer(stat, stat_ss, stat_rs, q).wait_recv())
    summed = jnp.sum(stat[...], axis=0)
    totals = jnp.concatenate([summed[i : i + 1] for i in range(packs)], axis=1)
    squares = jnp.concatenate([summed[packs + i : packs + i + 1] for i in range(packs)], axis=1)
    mean_dosage = totals / total_samples
    variance = squares / total_samples - mean_dosage * mean_dosage
    scale = lax.rsqrt(variance + EPSILON)
    for c in range(tiles):
        dosage = g_buf[c].astype(jnp.float32)
        x_ref[c] = ((dosage - mean_dosage) * scale).astype(jnp.bfloat16)
    each_peer(lambda q: to_peer(stat, stat_ss, stat_rs, q).wait_send())

    def t_copy(k, g, j, ahead):
        side = 0 if ahead else 1
        return pltpu.make_async_remote_copy(
            src_ref=t_own.at[g, j],
            dst_ref=t_side.at[g, side, j],
            send_sem=t_ss.at[k, g, side, j],
            recv_sem=t_rs.at[k, g, side, j],
            device_id=(me, mv + 1 if ahead else mv - 1),
            device_id_type=MESH,
        )

    @pl.when(mv == 0)
    def _():
        for g in range(GROUPS):
            t_side[g, 0] = jnp.zeros(t_side.shape[2:], t_side.dtype)

    @pl.when(mv == nv - 1)
    def _():
        for g in range(GROUPS):
            t_side[g, 1] = jnp.zeros(t_side.shape[2:], t_side.dtype)

    def row_sums(first, second):
        return jnp.sum(first * second, axis=1, keepdims=True)

    traits = u_hl.shape[1] // 2
    chunks = u_hl.shape[0]
    per_chunk = traits // kd

    def rows_at(c):
        return pl.ds(pl.multiple_of(c * traits, traits), traits)

    def project(k, g):
        end_gather(k, g)

        def decode(c):
            coded = u_all[g, pl.ds(c * per_chunk, per_chunk)].astype(jnp.int32)
            coded = coded.astype(jnp.float32).reshape(traits, width + LANES)
            u_hl[c] = split_high_low(coded[:, :width])
            u_scale[c] = jnp.broadcast_to(decoded_scale(coded[:, width:]), (traits, LANES))

        loop(chunks, decode)

        def products(j):
            def one(c):
                if k == 0:
                    both = lax.dot_general(
                        u_hl[c],
                        x_ref[j],
                        (((1,), (1,)), ((), ())),
                        preferred_element_type=jnp.float32,
                    )
                else:
                    both = jnp.dot(u_hl[c], xt_ref[j], preferred_element_type=jnp.float32)
                t_own[g, j, rows_at(c)] = (
                    (both[:traits] + both[traits:]) * u_scale[c, :, 0:1]
                ).astype(jnp.bfloat16)

            loop(chunks, one)

            @pl.when(mv < nv - 1)
            def _():
                t_copy(k, g, j, True).start()

            @pl.when(mv > 0)
            def _():
                t_copy(k, g, j, False).start()

        loop(tiles, products)

    def pair_copy(k, f, side):
        return pltpu.make_async_remote_copy(
            src_ref=slot_of(p_send, f, side),
            dst_ref=p_pair.at[f],
            send_sem=pair_ss.at[k, f],
            recv_sem=pair_rs.at[k, f],
            device_id=(partner, mv),
            device_id_type=MESH,
        )

    def p_copy(k, f, place):
        return pltpu.make_async_remote_copy(
            src_ref=slot_of(p_send, f, parity),
            dst_ref=p_recv.at[place],
            send_sem=p_ss.at[k, f],
            recv_sem=p_rs.at[k, place],
            device_id=(2 * f + parity, mv),
            device_id_type=MESH,
        )

    def project_back(k, g):
        def back(j):
            @pl.when(mv > 0)
            def _():
                t_copy(k, g, j, True).wait_recv()

            @pl.when(mv < nv - 1)
            def _():
                t_copy(k, g, j, False).wait_recv()

            def one(c):
                at = rows_at(c)
                sides = t_side[g, 0, j, at].astype(jnp.float32) + t_side[g, 1, j, at].astype(
                    jnp.float32
                )
                mixed = t_own[g, j, at].astype(jnp.float32) + 0.5 * sides
                forms = lax.dot_general(
                    jnp.ones((8, ROWS), jnp.bfloat16),
                    split_high_low(t_own[g, j, at].astype(jnp.float32) * mixed),
                    (((1,), (1,)), ((), ())),
                    preferred_element_type=jnp.float32,
                )
                form = forms[:, :traits] + forms[:, traits:]
                if isinstance(j, int) and j == 0:
                    block_forms[k, mv, c] = form
                else:
                    block_forms[k, mv, c] = block_forms[k, mv, c] + form
                part = jnp.dot(
                    mixed.astype(jnp.bfloat16), x_ref[j], preferred_element_type=jnp.float32
                )
                if isinstance(j, int) and j == 0:
                    p_acc[at] = part
                else:
                    p_acc[at] = p_acc[at] + part

            loop(chunks, one)

        if tiles > 4:
            p_acc[...] = jnp.zeros_like(p_acc)
            block_forms[k, mv] = jnp.zeros(block_forms.shape[2:], jnp.float32)
        loop(tiles, back)

        def to_send(c):
            pieces, _ = encode(p_acc[rows_at(c)] * (1.0 / total_samples))
            p_send[g, pl.ds(c * per_chunk, per_chunk)] = pieces.reshape(
                per_chunk, kd, width + LANES
            )

        loop(chunks, to_send)
        gather_sent(k, g)
        each_member(g, lambda f: pair_copy(k, f, 1 - parity).start())
        each_block(lambda q: across_blocks(block_forms, bf_ss, bf_rs, k, mv, q).start())

        def t_sent(j):
            @pl.when(mv < nv - 1)
            def _():
                t_copy(k, g, j, True).wait_send()

            @pl.when(mv > 0)
            def _():
                t_copy(k, g, j, False).wait_send()

        loop(tiles, t_sent)

    def add_pairs(k, g):
        def add(f):
            pair_copy(k, f, parity).wait_recv()
            held = slot_of(p_send, f, parity)
            held[...], _ = encode(decode_rows(held[...]) + decode_rows(p_pair[f]))

            @pl.when(f != mine)
            def _():
                p_copy(k, f, mine).start()

            @pl.when(f == mine)
            def _():
                p_recv[mine] = held[...]

        each_member(g, add)

    def across_blocks(buf, ss, rs, k, slot, peer):
        return pltpu.make_async_remote_copy(
            src_ref=buf.at[k, slot],
            dst_ref=buf.at[k, slot],
            send_sem=ss.at[k, peer],
            recv_sem=rs.at[k, slot],
            device_id=(me, peer),
            device_id_type=MESH,
        )

    def across_samples(k, slot, peer):
        return pltpu.make_async_remote_copy(
            src_ref=sample_forms.at[k, slot],
            dst_ref=sample_forms.at[k, slot],
            send_sem=sf_ss.at[k, peer],
            recv_sem=sf_rs.at[k, slot],
            device_id=(peer, mv),
            device_id_type=MESH,
        )

    def each_block(action):
        loop(nv - 1, lambda i: action(lax.rem(mv + i + 1, nv)))

    def send_norm(k):
        residual = res_ref[...]
        norms[k, mv] = jnp.broadcast_to(row_sums(residual, residual), (kd, LANES))
        each_block(lambda q: across_blocks(norms, norm_ss, norm_rs, k, mv, q).start())

    def send_forms(k):
        each_block(lambda q: across_blocks(block_forms, bf_ss, bf_rs, k, q, q).wait_recv())
        sample_forms[k, me] = jnp.sum(block_forms[k], axis=0)
        each_peer(lambda q: across_samples(k, me, q).start())

    def norm_of(k):
        each_block(lambda q: across_blocks(norms, norm_ss, norm_rs, k, q, q).wait_recv())
        return jnp.sum(norms[k], axis=0)[:, 0:1]

    def own_form(k):
        each_peer(lambda q: across_samples(k, q, q).wait_recv())
        forms = jnp.sum(sample_forms[k], axis=0)
        row = lax.broadcasted_iota(jnp.int32, (kd, traits), 0)
        column = lax.broadcasted_iota(jnp.int32, (kd, traits), 1)
        found = jnp.zeros((kd, traits), jnp.float32)
        for c in range(chunks):
            wanted = me * kd + row - c * traits
            found = found + jnp.where(column == wanted, forms[c, 0:1, :], 0.0)
        return jnp.sum(found, axis=1, keepdims=True)

    def update(k, before):
        norm = norm_of(k)
        form = own_form(k) * (1.0 / total_samples) + RIDGE * norm
        each_far(lambda f: p_copy(k, f, f).wait_recv())
        linked = decode_rows(p_recv[0])
        for f in range(1, pairs):
            linked = linked + decode_rows(p_recv[f])
        residual = res_ref[...]
        if before is None:
            step = norm / form
            direction = residual
        else:
            last_norm, last_step = before
            ratio = norm / last_norm
            step = norm / (form - ratio * norm / last_step)
            direction = residual + ratio * dir_ref[...]
            linked = linked + ratio * link_ref[...]
        if k + 1 < ITERS:
            image = mask_row * linked + RIDGE * direction
            my_slot[...], res_ref[...] = encode(residual - step * image)
            start_gather(k + 1)
            send_norm(k + 1)
            dir_ref[...] = direction
            link_ref[...] = linked
            sol_ref[...] = sol_ref[...] + step * direction
            imp_ref[...] = imp_ref[...] + step * linked
        else:
            sol_ref[...] = sol_ref[...] + step * direction
            projected = imp_ref[...] + step * linked
            imp_ref[...] = jnp.where(mask_ref[...] == 1, z_ref[...], projected)
        return norm, step

    def finish(k, g):
        each_member(g, lambda f: pair_copy(k, f, 1 - parity).wait_send())

        def sent(f):
            @pl.when(f != mine)
            def _():
                p_copy(k, f, mine).wait_send()

        each_member(g, sent)
        each_block(lambda q: across_blocks(block_forms, bf_ss, bf_rs, k, mv, q).wait_send())
        each_block(lambda q: across_blocks(norms, norm_ss, norm_rs, k, mv, q).wait_send())
        each_peer(lambda q: across_samples(k, me, q).wait_send())

    def transpose(j):
        xt_ref[j] = x_ref[j].T

    groups = range(GROUPS)
    before = None
    send_norm(0)
    for k in range(ITERS):
        for g in groups:
            project(k, g)
        for g in groups:
            project_back(k, g)
        if k == 0:
            loop(tiles // 2, transpose)
        for g in groups:
            add_pairs(k, g)
        send_forms(k)
        if k == 0:
            loop(tiles - tiles // 2, lambda j: transpose(tiles // 2 + j))
        before = update(k, before)
        for g in groups:
            finish(k, g)


def on_device(genotypes, typed_mask, z_scores):
    n, nv = lax.axis_size("samples"), lax.axis_size("vblocks")
    samples_dev, width = genotypes.shape
    kd = z_scores.shape[0]
    group_traits = n * kd // GROUPS
    tiles = samples_dev // ROWS
    vmem = pl.BlockSpec(memory_space=pltpu.VMEM)
    dma = pltpu.SemaphoreType.DMA
    out = jax.ShapeDtypeStruct((kd, width), jnp.float32)
    return pl.pallas_call(
        functools.partial(kernel, n, nv),
        out_shape=(out, out),
        in_specs=[pl.BlockSpec(memory_space=pl.ANY), vmem, vmem],
        out_specs=(vmem, vmem),
        scratch_shapes=[
            pltpu.VMEM((tiles, ROWS, width), jnp.int32),
            pltpu.VMEM((tiles, ROWS, width), jnp.bfloat16),
            pltpu.VMEM((tiles, width, ROWS), jnp.bfloat16),
            pltpu.VMEM((n, 2 * width // LANES, LANES), jnp.float32),
            pltpu.VMEM((GROUPS, n // GROUPS, kd, width + LANES), jnp.int16),
            pltpu.VMEM((group_traits // TRAITS, 2 * TRAITS, width), jnp.bfloat16),
            pltpu.VMEM((group_traits // TRAITS, TRAITS, LANES), jnp.float32),
            pltpu.VMEM((kd, width), jnp.float32),
            pltpu.VMEM((kd, width), jnp.float32),
            pltpu.VMEM((kd, width), jnp.float32),
            pltpu.VMEM((GROUPS, tiles, group_traits, ROWS), jnp.bfloat16),
            pltpu.VMEM((GROUPS, 2, tiles, group_traits, ROWS), jnp.bfloat16),
            pltpu.VMEM((group_traits, width), jnp.float32),
            pltpu.VMEM((GROUPS, n // GROUPS, kd, width + LANES), jnp.int16),
            pltpu.VMEM((n // 2, kd, width + LANES), jnp.int16),
            pltpu.VMEM((n // 2, kd, width + LANES), jnp.int16),
            pltpu.VMEM((ITERS, nv, kd, LANES), jnp.float32),
            pltpu.VMEM((ITERS, nv, n * kd // TRAITS, 8, TRAITS), jnp.float32),
            pltpu.VMEM((ITERS, n, n * kd // TRAITS, 8, TRAITS), jnp.float32),
            dma((tiles,)),
            dma((n,)),
            dma((n,)),
            dma((ITERS, 2, n // 2)),
            dma((ITERS, n)),
            dma((ITERS, GROUPS, 2, tiles)),
            dma((ITERS, GROUPS, 2, tiles)),
            dma((ITERS, n // 2)),
            dma((ITERS, n // 2)),
            dma((ITERS, n // 2)),
            dma((ITERS, n // 2)),
            dma((ITERS, nv)),
            dma((ITERS, nv)),
            dma((ITERS, nv)),
            dma((ITERS, nv)),
            dma((ITERS, n)),
            dma((ITERS, n)),
        ],
        compiler_params=pltpu.CompilerParams(
            collective_id=0, has_side_effects=True, vmem_limit_bytes=56 << 20
        ),
    )(genotypes, typed_mask[None, :], z_scores)


def solution(mesh):
    placed = (P("samples", "vblocks"), P("vblocks"), P("samples", "vblocks"))
    return jax.shard_map(
        on_device,
        mesh=mesh,
        in_specs=placed,
        out_specs=(P("samples", "vblocks"), P("samples", "vblocks")),
        check_vma=False,
    )
```

```python
import functools

import jax
import jax.numpy as jnp
from jax import lax
from jax.experimental import pallas as pl
from jax.experimental.pallas import tpu as pltpu
from jax.sharding import PartitionSpec as P

ITERS = 3
RIDGE = 0.1
EPSILON = 1e-05
MESH = pl.DeviceIdType.MESH
ROWS = 256
TRAITS = 128
GROUPS = 1
LANES = 128


def loop(count, body):
    if count <= 4:
        for index in range(count):
            body(index)
    else:
        lax.fori_loop(0, count, lambda index, carry: (body(index), carry)[1], 0)


def split_high_low(value):
    high = value.astype(jnp.bfloat16)
    low = (value - high.astype(jnp.float32)).astype(jnp.bfloat16)
    return jnp.concatenate([high, low], axis=0)


LEVELS = 32000.0


def decoded_scale(digits):
    return digits[:, 0:1] * jnp.exp2(digits[:, 1:2] - 13.0)


def encode(value):
    rows = value.shape[0]
    biggest = jnp.max(jnp.abs(value), axis=1, keepdims=True)
    wanted = jnp.maximum(biggest, 1e-28) * (1.0 / LEVELS)
    exponent = jnp.floor(jnp.log2(wanted))
    mantissa = jnp.ceil(wanted * jnp.exp2(13.0 - exponent))
    lane = lax.broadcasted_iota(jnp.int32, (rows, LANES), 1)
    digits = jnp.where(lane == 0, mantissa, jnp.where(lane == 1, exponent, 0.0))
    scale = decoded_scale(digits)
    coded = jnp.round(value * (1.0 / scale))
    both = jnp.concatenate([coded, digits], axis=1).astype(jnp.int32).astype(jnp.int16)
    return both, coded * scale


def decode_rows(both):
    both = both.astype(jnp.int32).astype(jnp.float32)
    width = both.shape[1] - LANES
    return both[:, :width] * decoded_scale(both[:, width:])


def kernel(
    n,
    nv,
    g_hbm,
    mask_ref,
    z_ref,
    sol_ref,
    imp_ref,
    g_buf,
    x_ref,
    xt_ref,
    stat,
    u_all,
    u_hl,
    u_scale,
    res_ref,
    dir_ref,
    link_ref,
    t_own,
    t_side,
    p_acc,
    form_acc,
    p_send,
    p_pair,
    p_recv,
    norms,
    block_forms,
    sample_forms,
    g_sem,
    stat_ss,
    stat_rs,
    u_ss,
    u_rs,
    t_ss,
    t_rs,
    pair_ss,
    pair_rs,
    p_ss,
    p_rs,
    norm_ss,
    norm_rs,
    bf_ss,
    bf_rs,
    sf_ss,
    sf_rs,
):
    me = lax.axis_index("samples")
    mv = lax.axis_index("vblocks")
    tiles, _, width = g_buf.shape
    kd = z_ref.shape[0]
    packs = width // LANES
    total_samples = float(n * tiles * ROWS)

    for c in range(tiles):
        pltpu.make_async_copy(
            g_hbm.at[pl.ds(c * ROWS, ROWS)], g_buf.at[c], g_sem.at[c]
        ).start()

    barrier = pltpu.get_barrier_semaphore()

    def greet_samples(i):
        peer = lax.rem(me + i + 1, n)
        pl.semaphore_signal(barrier, inc=1, device_id=(peer, mv), device_id_type=MESH)

    def greet_blocks(i):
        peer = lax.rem(mv + i + 1, nv)
        pl.semaphore_signal(barrier, inc=1, device_id=(me, peer), device_id_type=MESH)

    loop(n - 1, greet_samples)
    loop(nv - 1, greet_blocks)

    def to_peer(buf, ss, rs, peer):
        return pltpu.make_async_remote_copy(
            src_ref=buf.at[me],
            dst_ref=buf.at[me],
            send_sem=ss.at[peer],
            recv_sem=rs.at[me],
            device_id=(peer, mv),
            device_id_type=MESH,
        )

    def from_peer(buf, ss, rs, peer):
        return pltpu.make_async_remote_copy(
            src_ref=buf.at[peer],
            dst_ref=buf.at[peer],
            send_sem=ss.at[peer],
            recv_sem=rs.at[peer],
            device_id=(peer, mv),
            device_id_type=MESH,
        )

    def each_peer(action):
        loop(n - 1, lambda i: action(lax.rem(me + i + 1, n)))

    mine, parity = me // 2, lax.rem(me, 2)
    partner = me + 1 - 2 * parity
    pairs = n // 2
    my_group = lax.rem(mine, GROUPS)
    members = pairs // GROUPS

    def each_far(action):
        loop(pairs - 1, lambda i: action(lax.rem(mine + i + 1, pairs)))

    def each_member(g, action):
        start = mine // GROUPS + 1
        loop(members, lambda i: action(GROUPS * lax.rem(start + i, members) + g))

    def slot_of(ref, f, side):
        return ref.at[lax.rem(f, GROUPS), 2 * (f // GROUPS) + side]

    def far_copy(k, f, target):
        return pltpu.make_async_remote_copy(
            src_ref=slot_of(u_all, f, parity),
            dst_ref=slot_of(u_all, f, parity),
            send_sem=u_ss.at[k, 0, target],
            recv_sem=u_rs.at[k, 2 * f + parity],
            device_id=(2 * target + parity, mv),
            device_id_type=MESH,
        )

    def partner_copy(k, f, side):
        return pltpu.make_async_remote_copy(
            src_ref=slot_of(u_all, f, side),
            dst_ref=slot_of(u_all, f, side),
            send_sem=u_ss.at[k, 1, f],
            recv_sem=u_rs.at[k, 2 * f + side],
            device_id=(partner, mv),
            device_id_type=MESH,
        )

    def start_gather(k):
        each_far(lambda f: far_copy(k, mine, f).start())
        partner_copy(k, mine, parity).start()

    def end_gather(k, g):
        def forward(f):
            @pl.when(f != mine)
            def _():
                far_copy(k, f, f).wait_recv()
                partner_copy(k, f, parity).start()

        each_member(g, forward)
        each_member(g, lambda f: partner_copy(k, f, 1 - parity).wait_recv())

    def gather_sent(k, g):
        @pl.when(my_group == g)
        def _():
            each_far(lambda f: far_copy(k, mine, f).wait_send())

        each_member(g, lambda f: partner_copy(k, f, parity).wait_send())

    totals = jnp.zeros((1, width), jnp.float32)
    squares = jnp.zeros((1, width), jnp.float32)
    for c in range(tiles):
        pltpu.make_async_copy(
            g_hbm.at[pl.ds(c * ROWS, ROWS)], g_buf.at[c], g_sem.at[c]
        ).wait()
        dosage = g_buf[c].astype(jnp.float32)
        totals = totals + jnp.sum(dosage, axis=0, keepdims=True)
        squares = squares + jnp.sum(dosage * dosage, axis=0, keepdims=True)
    for i in range(packs):
        stat[me, i : i + 1, :] = totals[:, i * LANES : (i + 1) * LANES]
        stat[me, packs + i : packs + i + 1, :] = squares[:, i * LANES : (i + 1) * LANES]
    mask_row = mask_ref[...].astype(jnp.float32)
    residual = mask_row * z_ref[...]
    my_slot = slot_of(u_all, mine, parity)
    my_slot[...], res_ref[...] = encode(residual)
    dir_ref[...] = jnp.zeros_like(residual)
    link_ref[...] = jnp.zeros_like(residual)
    sol_ref[...] = jnp.zeros_like(residual)
    imp_ref[...] = jnp.zeros_like(residual)

    pl.semaphore_wait(barrier, n - 1 + nv - 1)
    each_peer(lambda q: to_peer(stat, stat_ss, stat_rs, q).start())
    start_gather(0)
    each_peer(lambda q: from_peer(stat, stat_ss, stat_rs, q).wait_recv())
    summed = jnp.sum(stat[...], axis=0)
    totals = jnp.concatenate([summed[i : i + 1] for i in range(packs)], axis=1)
    squares = jnp.concatenate([summed[packs + i : packs + i + 1] for i in range(packs)], axis=1)
    mean_dosage = totals / total_samples
    variance = squares / total_samples - mean_dosage * mean_dosage
    scale = lax.rsqrt(variance + EPSILON)
    for c in range(tiles):
        dosage = g_buf[c].astype(jnp.float32)
        x_ref[c] = ((dosage - mean_dosage) * scale).astype(jnp.bfloat16)
    each_peer(lambda q: to_peer(stat, stat_ss, stat_rs, q).wait_send())

    def t_copy(k, g, j, ahead):
        side = 0 if ahead else 1
        return pltpu.make_async_remote_copy(
            src_ref=t_own.at[g, j],
            dst_ref=t_side.at[g, side, j],
            send_sem=t_ss.at[k, g, side, j],
            recv_sem=t_rs.at[k, g, side, j],
            device_id=(me, mv + 1 if ahead else mv - 1),
            device_id_type=MESH,
        )

    @pl.when(mv == 0)
    def _():
        for g in range(GROUPS):
            t_side[g, 0] = jnp.zeros(t_side.shape[2:], t_side.dtype)

    @pl.when(mv == nv - 1)
    def _():
        for g in range(GROUPS):
            t_side[g, 1] = jnp.zeros(t_side.shape[2:], t_side.dtype)

    def row_sums(first, second):
        return jnp.sum(first * second, axis=1, keepdims=True)

    traits = u_hl.shape[1] // 2
    chunks = u_hl.shape[0]
    per_chunk = traits // kd

    def rows_at(c):
        return pl.ds(pl.multiple_of(c * traits, traits), traits)

    def project(k, g):
        end_gather(k, g)

        def decode(c):
            coded = u_all[g, pl.ds(c * per_chunk, per_chunk)].astype(jnp.int32)
            coded = coded.astype(jnp.float32).reshape(traits, width + LANES)
            u_hl[c] = split_high_low(coded[:, :width])
            u_scale[c] = jnp.broadcast_to(decoded_scale(coded[:, width:]), (traits, LANES))

        loop(chunks, decode)

        def products(j):
            def one(c):
                if k == 0:
                    both = lax.dot_general(
                        u_hl[c],
                        x_ref[j],
                        (((1,), (1,)), ((), ())),
                        preferred_element_type=jnp.float32,
                    )
                else:
                    both = jnp.dot(u_hl[c], xt_ref[j], preferred_element_type=jnp.float32)
                t_own[g, j, rows_at(c)] = (
                    (both[:traits] + both[traits:]) * u_scale[c, :, 0:1]
                ).astype(jnp.bfloat16)

            loop(chunks, one)

            @pl.when(mv < nv - 1)
            def _():
                t_copy(k, g, j, True).start()

            @pl.when(mv > 0)
            def _():
                t_copy(k, g, j, False).start()

        loop(tiles, products)

    def pair_copy(k, f, side):
        return pltpu.make_async_remote_copy(
            src_ref=slot_of(p_send, f, side),
            dst_ref=p_pair.at[f],
            send_sem=pair_ss.at[k, f],
            recv_sem=pair_rs.at[k, f],
            device_id=(partner, mv),
            device_id_type=MESH,
        )

    def p_copy(k, f, place):
        return pltpu.make_async_remote_copy(
            src_ref=slot_of(p_send, f, parity),
            dst_ref=p_recv.at[place],
            send_sem=p_ss.at[k, f],
            recv_sem=p_rs.at[k, place],
            device_id=(2 * f + parity, mv),
            device_id_type=MESH,
        )

    def project_back(k, g):
        def back(j):
            @pl.when(mv > 0)
            def _():
                t_copy(k, g, j, True).wait_recv()

            @pl.when(mv < nv - 1)
            def _():
                t_copy(k, g, j, False).wait_recv()

            def one(c):
                at = rows_at(c)
                sides = t_side[g, 0, j, at].astype(jnp.float32) + t_side[g, 1, j, at].astype(
                    jnp.float32
                )
                mixed = t_own[g, j, at].astype(jnp.float32) + 0.5 * sides
                product = t_own[g, j, at].astype(jnp.float32) * mixed
                if isinstance(j, int) and j == 0:
                    form_acc[at] = product
                else:
                    form_acc[at] = form_acc[at] + product
                part = jnp.dot(
                    mixed.astype(jnp.bfloat16), x_ref[j], preferred_element_type=jnp.float32
                )
                if isinstance(j, int) and j == 0:
                    p_acc[at] = part
                else:
                    p_acc[at] = p_acc[at] + part

            loop(chunks, one)

        if tiles > 4:
            p_acc[...] = jnp.zeros_like(p_acc)
            form_acc[...] = jnp.zeros_like(form_acc)
        loop(tiles, back)

        def to_send(c):
            pieces, _ = encode(p_acc[rows_at(c)] * (1.0 / total_samples))
            p_send[g, pl.ds(c * per_chunk, per_chunk)] = pieces.reshape(
                per_chunk, kd, width + LANES
            )

        loop(chunks, to_send)
        gather_sent(k, g)
        each_member(g, lambda f: pair_copy(k, f, 1 - parity).start())

        def sum_forms(c):
            forms = lax.dot_general(
                jnp.ones((8, ROWS), jnp.bfloat16),
                split_high_low(form_acc[rows_at(c)]),
                (((1,), (1,)), ((), ())),
                preferred_element_type=jnp.float32,
            )
            block_forms[k, mv, c] = forms[:, :traits] + forms[:, traits:]

        loop(chunks, sum_forms)
        each_block(lambda q: across_blocks(block_forms, bf_ss, bf_rs, k, mv, q).start())

        def t_sent(j):
            @pl.when(mv < nv - 1)
            def _():
                t_copy(k, g, j, True).wait_send()

            @pl.when(mv > 0)
            def _():
                t_copy(k, g, j, False).wait_send()

        loop(tiles, t_sent)

    def add_pairs(k, g):
        def add(f):
            pair_copy(k, f, parity).wait_recv()
            held = slot_of(p_send, f, parity)
            held[...], _ = encode(decode_rows(held[...]) + decode_rows(p_pair[f]))

            @pl.when(f != mine)
            def _():
                p_copy(k, f, mine).start()

            @pl.when(f == mine)
            def _():
                p_recv[mine] = held[...]

        each_member(g, add)

    def across_blocks(buf, ss, rs, k, slot, peer):
        return pltpu.make_async_remote_copy(
            src_ref=buf.at[k, slot],
            dst_ref=buf.at[k, slot],
            send_sem=ss.at[k, peer],
            recv_sem=rs.at[k, slot],
            device_id=(me, peer),
            device_id_type=MESH,
        )

    def across_samples(k, slot, peer):
        return pltpu.make_async_remote_copy(
            src_ref=sample_forms.at[k, slot],
            dst_ref=sample_forms.at[k, slot],
            send_sem=sf_ss.at[k, peer],
            recv_sem=sf_rs.at[k, slot],
            device_id=(peer, mv),
            device_id_type=MESH,
        )

    def each_block(action):
        loop(nv - 1, lambda i: action(lax.rem(mv + i + 1, nv)))

    def send_norm(k):
        residual = res_ref[...]
        norms[k, mv] = jnp.broadcast_to(row_sums(residual, residual), (kd, LANES))
        each_block(lambda q: across_blocks(norms, norm_ss, norm_rs, k, mv, q).start())

    def send_forms(k):
        each_block(lambda q: across_blocks(block_forms, bf_ss, bf_rs, k, q, q).wait_recv())
        sample_forms[k, me] = jnp.sum(block_forms[k], axis=0)
        each_peer(lambda q: across_samples(k, me, q).start())

    def norm_of(k):
        each_block(lambda q: across_blocks(norms, norm_ss, norm_rs, k, q, q).wait_recv())
        return jnp.sum(norms[k], axis=0)[:, 0:1]

    def own_form(k):
        each_peer(lambda q: across_samples(k, q, q).wait_recv())
        forms = jnp.sum(sample_forms[k], axis=0)
        row = lax.broadcasted_iota(jnp.int32, (kd, traits), 0)
        column = lax.broadcasted_iota(jnp.int32, (kd, traits), 1)
        found = jnp.zeros((kd, traits), jnp.float32)
        for c in range(chunks):
            wanted = me * kd + row - c * traits
            found = found + jnp.where(column == wanted, forms[c, 0:1, :], 0.0)
        return jnp.sum(found, axis=1, keepdims=True)

    def update(k, before):
        norm = norm_of(k)
        form = own_form(k) * (1.0 / total_samples) + RIDGE * norm
        each_far(lambda f: p_copy(k, f, f).wait_recv())
        linked = decode_rows(p_recv[0])
        for f in range(1, pairs):
            linked = linked + decode_rows(p_recv[f])
        residual = res_ref[...]
        if before is None:
            step = norm / form
            direction = residual
        else:
            last_norm, last_step = before
            ratio = norm / last_norm
            step = norm / (form - ratio * norm / last_step)
            direction = residual + ratio * dir_ref[...]
            linked = linked + ratio * link_ref[...]
        if k + 1 < ITERS:
            image = mask_row * linked + RIDGE * direction
            my_slot[...], res_ref[...] = encode(residual - step * image)
            start_gather(k + 1)
            send_norm(k + 1)
            dir_ref[...] = direction
            link_ref[...] = linked
            sol_ref[...] = sol_ref[...] + step * direction
            imp_ref[...] = imp_ref[...] + step * linked
        else:
            sol_ref[...] = sol_ref[...] + step * direction
            projected = imp_ref[...] + step * linked
            imp_ref[...] = jnp.where(mask_ref[...] == 1, z_ref[...], projected)
        return norm, step

    def finish(k, g):
        each_member(g, lambda f: pair_copy(k, f, 1 - parity).wait_send())

        def sent(f):
            @pl.when(f != mine)
            def _():
                p_copy(k, f, mine).wait_send()

        each_member(g, sent)
        each_block(lambda q: across_blocks(block_forms, bf_ss, bf_rs, k, mv, q).wait_send())
        each_block(lambda q: across_blocks(norms, norm_ss, norm_rs, k, mv, q).wait_send())
        each_peer(lambda q: across_samples(k, me, q).wait_send())

    def transpose(j):
        xt_ref[j] = x_ref[j].T

    groups = range(GROUPS)
    before = None
    send_norm(0)
    for k in range(ITERS):
        for g in groups:
            project(k, g)
        for g in groups:
            project_back(k, g)
        if k == 0:
            loop(tiles // 2, transpose)
        for g in groups:
            add_pairs(k, g)
        send_forms(k)
        if k == 0:
            loop(tiles - tiles // 2, lambda j: transpose(tiles // 2 + j))
        before = update(k, before)
        for g in groups:
            finish(k, g)


def on_device(genotypes, typed_mask, z_scores):
    n, nv = lax.axis_size("samples"), lax.axis_size("vblocks")
    samples_dev, width = genotypes.shape
    kd = z_scores.shape[0]
    group_traits = n * kd // GROUPS
    tiles = samples_dev // ROWS
    vmem = pl.BlockSpec(memory_space=pltpu.VMEM)
    dma = pltpu.SemaphoreType.DMA
    out = jax.ShapeDtypeStruct((kd, width), jnp.float32)
    return pl.pallas_call(
        functools.partial(kernel, n, nv),
        out_shape=(out, out),
        in_specs=[pl.BlockSpec(memory_space=pl.ANY), vmem, vmem],
        out_specs=(vmem, vmem),
        scratch_shapes=[
            pltpu.VMEM((tiles, ROWS, width), jnp.int32),
            pltpu.VMEM((tiles, ROWS, width), jnp.bfloat16),
            pltpu.VMEM((tiles, width, ROWS), jnp.bfloat16),
            pltpu.VMEM((n, 2 * width // LANES, LANES), jnp.float32),
            pltpu.VMEM((GROUPS, n // GROUPS, kd, width + LANES), jnp.int16),
            pltpu.VMEM((group_traits // TRAITS, 2 * TRAITS, width), jnp.bfloat16),
            pltpu.VMEM((group_traits // TRAITS, TRAITS, LANES), jnp.float32),
            pltpu.VMEM((kd, width), jnp.float32),
            pltpu.VMEM((kd, width), jnp.float32),
            pltpu.VMEM((kd, width), jnp.float32),
            pltpu.VMEM((GROUPS, tiles, group_traits, ROWS), jnp.bfloat16),
            pltpu.VMEM((GROUPS, 2, tiles, group_traits, ROWS), jnp.bfloat16),
            pltpu.VMEM((group_traits, width), jnp.float32),
            pltpu.VMEM((group_traits, ROWS), jnp.float32),
            pltpu.VMEM((GROUPS, n // GROUPS, kd, width + LANES), jnp.int16),
            pltpu.VMEM((n // 2, kd, width + LANES), jnp.int16),
            pltpu.VMEM((n // 2, kd, width + LANES), jnp.int16),
            pltpu.VMEM((ITERS, nv, kd, LANES), jnp.float32),
            pltpu.VMEM((ITERS, nv, n * kd // TRAITS, 8, TRAITS), jnp.float32),
            pltpu.VMEM((ITERS, n, n * kd // TRAITS, 8, TRAITS), jnp.float32),
            dma((tiles,)),
            dma((n,)),
            dma((n,)),
            dma((ITERS, 2, n // 2)),
            dma((ITERS, n)),
            dma((ITERS, GROUPS, 2, tiles)),
            dma((ITERS, GROUPS, 2, tiles)),
            dma((ITERS, n // 2)),
            dma((ITERS, n // 2)),
            dma((ITERS, n // 2)),
            dma((ITERS, n // 2)),
            dma((ITERS, nv)),
            dma((ITERS, nv)),
            dma((ITERS, nv)),
            dma((ITERS, nv)),
            dma((ITERS, n)),
            dma((ITERS, n)),
        ],
        compiler_params=pltpu.CompilerParams(
            collective_id=0, has_side_effects=True, vmem_limit_bytes=56 << 20
        ),
    )(genotypes, typed_mask[None, :], z_scores)


def solution(mesh):
    placed = (P("samples", "vblocks"), P("vblocks"), P("samples", "vblocks"))
    return jax.shard_map(
        on_device,
        mesh=mesh,
        in_specs=placed,
        out_specs=(P("samples", "vblocks"), P("samples", "vblocks")),
        check_vma=False,
    )
```
